32 devices in a mesh: dp: 8 (over y, x, core), fsdp: 4 (over z).
Axes of the slice: x: 2, y: 2, z: 4, core: 2. Of those that a mesh axis runs over, the one named last changes fastest.
Arguments:
- tokens: bfloat16 [4096, 2560], P(('dp', 'fsdp')), may hold values from -6 to 6
- cotangent: bfloat16 [4096, 2560], P(('dp', 'fsdp')), may hold values from -6 to 6
- seq_lengths: int32 [32, 2], P(('dp', 'fsdp')), may hold values from 0 to 128, as said below
- wq_master: float32 [2560, 2560], P('dp', 'fsdp'), may hold values from -0.125 to 0.125
- wkv_master: float32 [2560, 512], P('dp', 'fsdp'), may hold values from -0.125 to 0.125
- wo_master: float32 [2560, 2560], P('dp', 'fsdp'), may hold values from -0.625 to 0.625
- ffw_up_master: float32 [2, 2560, 7680], P(None, 'dp', 'fsdp'), may hold values from -0.125 to 0.125
- ffw_down_master: float32 [7680, 2560], P('fsdp', 'dp'), may hold values from -0.0625 to 0.0625
- vec_master: float32 [4, 2560], P(None, ('dp', 'fsdp')), may hold values from -1.5 to 2.6
- wq_first: float32 [2560, 2560], P('dp', 'fsdp'), may hold values from -1 to 1
- wq_second: float32 [2560, 2560], P('dp', 'fsdp'), may hold values from 0 to 1
- wkv_first: float32 [2560, 512], P('dp', 'fsdp'), may hold values from -1 to 1
- wkv_second: float32 [2560, 512], P('dp', 'fsdp'), may hold values from 0 to 1
- wo_first: float32 [2560, 2560], P('dp', 'fsdp'), may hold values from -1 to 1
- wo_second: float32 [2560, 2560], P('dp', 'fsdp'), may hold values from 0 to 1
- ffw_up_first: float32 [2, 2560, 7680], P(None, 'dp', 'fsdp'), may hold values from -1 to 1
- ffw_up_second: float32 [2, 2560, 7680], P(None, 'dp', 'fsdp'), may hold values from 0 to 1
- ffw_down_first: float32 [7680, 2560], P('fsdp', 'dp'), may hold values from -1 to 1
- ffw_down_second: float32 [7680, 2560], P('fsdp', 'dp'), may hold values from 0 to 1
- vec_first: float32 [4, 2560], P(None, ('dp', 'fsdp')), may hold values from -1 to 1
- vec_second: float32 [4, 2560], P(None, ('dp', 'fsdp')), may hold values from 0 to 1
Outputs:
- block_out: bfloat16 [4096, 2560], P(('dp', 'fsdp'))
- input_grad: bfloat16 [4096, 2560], P(('dp', 'fsdp'))
- grad_norm: float32 [], replicated
- wq_clipped: float32 [2560, 2560], P('dp', 'fsdp')
- wq_first_new: float32 [2560, 2560], P('dp', 'fsdp')
- wq_second_new: float32 [2560, 2560], P('dp', 'fsdp')
- wq_updated: float32 [2560, 2560], P('dp', 'fsdp')
- wq_copy: bfloat16 [2560, 2560], P('dp', 'fsdp')
- wkv_clipped: float32 [2560, 512], P('dp', 'fsdp')
- wkv_first_new: float32 [2560, 512], P('dp', 'fsdp')
- wkv_second_new: float32 [2560, 512], P('dp', 'fsdp')
- wkv_updated: float32 [2560, 512], P('dp', 'fsdp')
- wkv_copy: bfloat16 [2560, 512], P('dp', 'fsdp')
- wo_clipped: float32 [2560, 2560], P('dp', 'fsdp')
- wo_first_new: float32 [2560, 2560], P('dp', 'fsdp')
- wo_second_new: float32 [2560, 2560], P('dp', 'fsdp')
- wo_updated: float32 [2560, 2560], P('dp', 'fsdp')
- wo_copy: bfloat16 [2560, 2560], P('dp', 'fsdp')
- ffw_up_clipped: float32 [2, 2560, 7680], P(None, 'dp', 'fsdp')
- ffw_up_first_new: float32 [2, 2560, 7680], P(None, 'dp', 'fsdp')
- ffw_up_second_new: float32 [2, 2560, 7680], P(None, 'dp', 'fsdp')
- ffw_up_updated: float32 [2, 2560, 7680], P(None, 'dp', 'fsdp')
- ffw_up_copy: bfloat16 [2, 2560, 7680], P(None, 'dp', 'fsdp')
- ffw_down_clipped: float32 [7680, 2560], P('fsdp', 'dp')
- ffw_down_first_new: float32 [7680, 2560], P('fsdp', 'dp')
- ffw_down_second_new: float32 [7680, 2560], P('fsdp', 'dp')
- ffw_down_updated: float32 [7680, 2560], P('fsdp', 'dp')
- ffw_down_copy: bfloat16 [7680, 2560], P('fsdp', 'dp')
- vec_clipped: float32 [4, 2560], P(None, ('dp', 'fsdp'))
- vec_first_new: float32 [4, 2560], P(None, ('dp', 'fsdp'))
- vec_second_new: float32 [4, 2560], P(None, ('dp', 'fsdp'))
- vec_updated: float32 [4, 2560], P(None, ('dp', 'fsdp'))
- vec_copy: bfloat16 [4, 2560], P(None, ('dp', 'fsdp'))
The draws below stay inside these ranges and needn't reach their ends.
Inputs may be any that keep to these rules, and one draw needn't show every extreme that they name: `seq_lengths`: row r lists the lengths of the sequences in buffer r in order, zeros after the last; slot 0 is never zero, every nonzero length is 64 or more, a row sums to at most 128, and some row holds one sequence of exactly 128 tokens.
All inputs are finite; a program needn't handle non-finite values.
Results may differ from the reference program's by a relative error of at most 0.02.
Values may be sent and summed in bfloat16 or wider, within the bound.
No kernel may reach another device: no remote copies, remote signals or barrier semaphores. Data moves between devices by JAX's collectives and lax.ppermute only.
A program may use at most 320 MiB of HBM per device.

```python
import math
import jax
import jax.numpy as jnp
from jax import lax

D = 2560
H = 10
HD = 256
FF = 7680
TOK_DEV = 128
MIN_LEN = 64
WINDOW = 2048
STEP = 5
SLOTS = 2
BUFFERS = 32
TOKENS = 4096
PARAMS = 73410560


Q_FACTOR = 1.3


KV_FACTOR = 6.1


O_FACTOR = 0.13


UP_FACTOR = 0.47


DOWN_FACTOR = 0.49


def unit_scale(factor):
    return factor / math.sqrt(PARAMS)


def normal_part(key, out_shape, magnitude):
    return magnitude * jax.random.truncated_normal(key, -4.0, 4.0, out_shape, jnp.float32)


def log_even(key, out_shape, lower):
    return lower * jnp.exp(jax.random.uniform(key, out_shape, jnp.float32, 0.0, math.log(4.0)))


def vector_scale():
    return jnp.array([[2.6], [0.8], [0.9], [0.45]], jnp.float32) / math.sqrt(PARAMS)


def draw_seq_lengths(key, part):
    key = jax.random.fold_in(key, 11)
    len_key, pick_key = jax.random.split(key)
    drawn = jax.random.randint(len_key, (BUFFERS, SLOTS), MIN_LEN, TOK_DEV + 1)
    running = jnp.cumsum(drawn, axis=1)
    lengths = jnp.where(running <= TOK_DEV, drawn, 0)
    chosen = jax.random.randint(pick_key, (), 0, BUFFERS)
    slot_ids = jnp.arange(SLOTS)
    full_row = jnp.where(slot_ids == 0, TOK_DEV, 0)
    lengths = jnp.where((jnp.arange(BUFFERS) == chosen)[:, None], full_row[None, :], lengths)
    return lengths.astype(jnp.int32)


def draw_vec_master(key, part):
    key = jax.random.fold_in(key, 3)
    gain_key, bias_key, gain_key_two, bias_key_two = jax.random.split(key, 4)
    ramp_up = jnp.arange(D, dtype=jnp.float32) / (D - 1)
    gain_row = (0.6 + 1.2 * ramp_up) * jax.random.uniform(gain_key, (D,), jnp.float32, 0.6, 1.4)
    bias_row = 0.5 * jax.random.truncated_normal(bias_key, -3.0, 3.0, (D,), jnp.float32)
    gain_row_two = (0.6 + 1.2 * ramp_up) * jax.random.uniform(gain_key_two, (D,), jnp.float32, 0.6, 1.4)
    bias_row_two = 0.5 * jax.random.truncated_normal(bias_key_two, -3.0, 3.0, (D,), jnp.float32)
    return jnp.stack([gain_row, bias_row, gain_row_two, bias_row_two]).astype(jnp.float32)


def draw_wq_first(key, part):
    key = jax.random.fold_in(key, 21)
    return normal_part(key, (D, H * HD), unit_scale(Q_FACTOR))


def draw_wq_second(key, part):
    key = jax.random.fold_in(key, 22)
    lower = unit_scale(Q_FACTOR) ** 2 / 3.0
    return log_even(key, (D, H * HD), lower)


def draw_wkv_first(key, part):
    key = jax.random.fold_in(key, 23)
    return normal_part(key, (D, 2 * HD), unit_scale(KV_FACTOR))


def draw_wkv_second(key, part):
    key = jax.random.fold_in(key, 24)
    lower = unit_scale(KV_FACTOR) ** 2 / 3.0
    return log_even(key, (D, 2 * HD), lower)


def draw_wo_first(key, part):
    key = jax.random.fold_in(key, 25)
    return normal_part(key, (H * HD, D), unit_scale(O_FACTOR))


def draw_wo_second(key, part):
    key = jax.random.fold_in(key, 26)
    lower = unit_scale(O_FACTOR) ** 2 / 3.0
    return log_even(key, (H * HD, D), lower)


def draw_ffw_up_first(key, part):
    key = jax.random.fold_in(key, 29)
    return normal_part(key, (2, D, FF), unit_scale(UP_FACTOR))


def draw_ffw_up_second(key, part):
    key = jax.random.fold_in(key, 30)
    lower = unit_scale(UP_FACTOR) ** 2 / 3.0
    return log_even(key, (2, D, FF), lower)


def draw_ffw_down_first(key, part):
    key = jax.random.fold_in(key, 31)
    return normal_part(key, (FF, D), unit_scale(DOWN_FACTOR))


def draw_ffw_down_second(key, part):
    key = jax.random.fold_in(key, 32)
    lower = unit_scale(DOWN_FACTOR) ** 2 / 3.0
    return log_even(key, (FF, D), lower)


def draw_vec_first(key, part):
    key = jax.random.fold_in(key, 27)
    return normal_part(key, (4, D), vector_scale())


def draw_vec_second(key, part):
    key = jax.random.fold_in(key, 28)
    lower = vector_scale() ** 2 / 3.0
    return log_even(key, (4, D), lower)


def with_spikes(values, key, source, target, parts, factor):
    def block_of(dim):
        return (jnp.arange(values.shape[dim]) // (values.shape[dim] // parts)).reshape((-1,) + (1,) * (values.ndim - 1 - dim))

    one_side = jax.random.permutation(key, parts)[block_of(target)]
    far = (block_of(target) + parts // 2) % parts
    return jnp.where((block_of(source) == one_side) | (block_of(source) == far), factor * values, values)


def levels(key, extent, cuts, smallest, top_value):
    def one(axis_at, shards_of):
        steps = jax.random.uniform(jax.random.fold_in(jax.random.fold_in(key, 6), axis_at), (shards_of,), jnp.float32, smallest / len(cuts), top_value / len(cuts))
        return jnp.repeat(jnp.exp(steps), extent[axis_at] // shards_of).reshape((-1,) + (1,) * (len(extent) - axis_at - 1))

    gain = one(*cuts[0])
    for cut in cuts[1:]:
        gain = gain * one(*cut)
    return gain


def normal_values(own_key, dims, spread, limit, cuts=(), kind=jnp.bfloat16):
    values = spread * jax.random.normal(own_key, dims, jnp.float32)
    if cuts:
        values = values * levels(own_key, dims, cuts, -0.22, 0.18)
    return jnp.clip(values, -limit, limit).astype(kind)


def bell_draw_with(stream_key, extent, deviation, limit, pieces, heavy, kind=jnp.bfloat16):
    entries = deviation * jax.random.normal(stream_key, extent, jnp.float32)
    if pieces:
        entries = entries * levels(stream_key, extent, pieces, -0.22, 0.18)
    return jnp.clip(with_spikes(entries, jax.random.fold_in(stream_key, 3), *heavy), -limit, limit).astype(kind)


def setup_inputs(seed: int = 0) -> dict:
    key_list = jax.random.split(jax.random.key(seed), 22)
    return {
        "tokens": normal_values(key_list[0], (TOKENS, D), 1.0, 6.0, ((0, 32),)),
        "cotangent": bell_draw_with(key_list[1], (TOKENS, D), 1.0, 6.0, ((0, 32),), (0, 1, 32, 2.75)),
        "seq_lengths": draw_seq_lengths(jax.random.fold_in(key_list[21], 71), 0),
        "wq_master": normal_values(key_list[3], (D, H * HD), D ** -0.5, 0.125, ((0, 8), (1, 4)), jnp.float32),
        "wkv_master": normal_values(key_list[4], (D, 2 * HD), D ** -0.5, 0.125, ((0, 8), (1, 4)), jnp.float32),
        "wo_master": normal_values(key_list[5], (H * HD, D), (H * HD // 32) ** -0.5, 0.625, ((0, 8), (1, 4)), jnp.float32),
        "ffw_up_master": normal_values(key_list[6], (2, D, FF), D ** -0.5, 0.125, ((1, 8), (2, 4)), jnp.float32),
        "ffw_down_master": normal_values(key_list[7], (FF, D), FF ** -0.5, 0.0625, ((0, 4), (1, 8)), jnp.float32),
        "vec_master": draw_vec_master(jax.random.fold_in(key_list[21], 71), 0),
        "wq_first": draw_wq_first(jax.random.fold_in(key_list[21], 71), 0),
        "wq_second": draw_wq_second(jax.random.fold_in(key_list[21], 71), 0),
        "wkv_first": draw_wkv_first(jax.random.fold_in(key_list[21], 71), 0),
        "wkv_second": draw_wkv_second(jax.random.fold_in(key_list[21], 71), 0),
        "wo_first": draw_wo_first(jax.random.fold_in(key_list[21], 71), 0),
        "wo_second": draw_wo_second(jax.random.fold_in(key_list[21], 71), 0),
        "ffw_up_first": draw_ffw_up_first(jax.random.fold_in(key_list[21], 71), 0),
        "ffw_up_second": draw_ffw_up_second(jax.random.fold_in(key_list[21], 71), 0),
        "ffw_down_first": draw_ffw_down_first(jax.random.fold_in(key_list[21], 71), 0),
        "ffw_down_second": draw_ffw_down_second(jax.random.fold_in(key_list[21], 71), 0),
        "vec_first": draw_vec_first(jax.random.fold_in(key_list[21], 71), 0),
        "vec_second": draw_vec_second(jax.random.fold_in(key_list[21], 71), 0),
    }


HIGHEST = lax.Precision.HIGHEST
EPS_NORM = 1e-06
ROPE_BASE = 10000.0
NEG_BIG = -1e+30
CLIP_NORM = 1.0
BETA_ONE = 0.5
BETA_TWO = 0.75
EPS_ADAM = 1e-08
DECAY_RATE = 0.1
LR_VECTOR = 0.3

@jax.custom_vjp
def low(v):
    return lax.optimization_barrier(v.astype(jnp.bfloat16)).astype(jnp.float32)

@jax.custom_vjp
def low_back(v):
    return v

def low_keep(v):
    return (low(v), None)

def low_pass(kept, grad):
    return (grad,)

def back_keep(v):
    return (v, None)

def back_low(kept, grad):
    return (low(grad),)
low.defvjp(low_keep, low_pass)
low_back.defvjp(back_keep, back_low)

def layout(lengths):
    places = jnp.arange(TOK_DEV, dtype=jnp.int32)
    end_at = jnp.cumsum(lengths).astype(jnp.int32)
    segment = lax.optimization_barrier(jnp.sum((places[:, None] >= end_at[None, :]).astype(jnp.int32), axis=1))
    slot_ids = jnp.arange(SLOTS, dtype=jnp.int32)
    start_of = lax.optimization_barrier(jnp.sum(jnp.where(segment[:, None] > slot_ids[None, :], lengths[None, :], 0), axis=1))
    position = places - start_of
    valid_mask = (places < end_at[SLOTS - 1]).astype(jnp.float32)
    return (places, segment, position, valid_mask)

def rotate(values, position, orient):
    half_dim = values.shape[-1] // 2
    quarter = half_dim // 2
    exponent = jnp.arange(quarter, dtype=jnp.float32) * (2.0 / half_dim)
    angles = position.astype(jnp.float32)[:, None] / (ROPE_BASE ** exponent)[None, :]
    cosine = jnp.cos(angles)[:, None, :]
    sine_vals = orient * jnp.sin(angles)[:, None, :]
    first_part = values[..., :quarter]
    second = values[..., quarter:half_dim]
    return jnp.concatenate([first_part * cosine - second * sine_vals, second * cosine + first_part * sine_vals, values[..., half_dim:]], axis=-1)

def glu_mix(gate_lin, up_lin):
    return jax.nn.gelu(gate_lin, approximate=True) * up_lin

def row_forward(low_weights, x_row, lengths):
    wq_low, wkv_low, wo_low, up_low, down_low, vec_low = low_weights
    places, segment, position, valid_mask = layout(lengths)
    gain_one = vec_low[0]
    bias_one = vec_low[1]
    gain_two = vec_low[2]
    bias_two = vec_low[3]
    mean_sq = lax.optimization_barrier(jnp.mean(x_row * x_row, axis=1, keepdims=True))
    normed = low(x_row * lax.rsqrt(mean_sq + EPS_NORM) * gain_one[None, :])
    q_lin = low_back(jnp.dot(normed, wq_low, precision=HIGHEST, preferred_element_type=jnp.float32))
    kv_lin = low_back(jnp.dot(normed, wkv_low, precision=HIGHEST, preferred_element_type=jnp.float32))
    queries = low(rotate(q_lin.reshape(TOK_DEV, H, HD), position, 1.0) * HD ** (-0.5))
    keys_rot = low(rotate(kv_lin[:, None, :HD], position, 1.0)[:, 0, :])
    values_low = low(kv_lin[:, HD:])
    scores = low_back(jnp.einsum('qhe,ke->hqk', queries, keys_rot, precision=HIGHEST))
    allowed = (segment[:, None] == segment[None, :]) & (places[None, :] <= places[:, None]) & (places[:, None] - places[None, :] < WINDOW)
    prob_low = low(jax.nn.softmax(jnp.where(allowed[None], scores, NEG_BIG), axis=-1))
    attended = jnp.einsum('hqk,ke->qhe', prob_low, values_low, precision=HIGHEST).reshape(TOK_DEV, H * HD)
    attended = low(low_back(attended))
    branch = jnp.dot(attended, wo_low, precision=HIGHEST, preferred_element_type=jnp.float32) + bias_one[None, :]
    mixed = x_row + low_back(valid_mask[:, None] * branch)
    mean_two = lax.optimization_barrier(jnp.mean(mixed * mixed, axis=1, keepdims=True))
    normed_two = low(mixed * lax.rsqrt(mean_two + EPS_NORM) * gain_two[None, :])
    gate_lin = low_back(jnp.dot(normed_two, up_low[0], precision=HIGHEST, preferred_element_type=jnp.float32))
    up_lin = low_back(jnp.dot(normed_two, up_low[1], precision=HIGHEST, preferred_element_type=jnp.float32))
    hidden = low(glu_mix(gate_lin, up_lin))
    branch_two = jnp.dot(hidden, down_low, precision=HIGHEST, preferred_element_type=jnp.float32) + bias_two[None, :]
    return mixed + valid_mask[:, None] * branch_two

def adamw(gradient, first_mom, second_mom, weight, factor, step_rate):
    clipped = gradient * factor
    first_new = BETA_ONE * first_mom + (1.0 - BETA_ONE) * clipped
    second_new = BETA_TWO * second_mom + (1.0 - BETA_TWO) * clipped * clipped
    first_hat = first_new / (1.0 - BETA_ONE ** STEP)
    second_hat = second_new / (1.0 - BETA_TWO ** STEP)
    weight_new = weight - step_rate * (first_hat / (jnp.sqrt(second_hat) + EPS_ADAM) + DECAY_RATE * weight)
    return (clipped, first_new, second_new, weight_new, weight_new.astype(jnp.bfloat16))

def valid_of(lengths):
    return layout(lengths)[3]

def reference(tokens, cotangent, seq_lengths, wq_master, wkv_master, wo_master, ffw_up_master, ffw_down_master, vec_master, wq_first, wq_second, wkv_first, wkv_second, wo_first, wo_second, ffw_up_first, ffw_up_second, ffw_down_first, ffw_down_second, vec_first, vec_second):
    x_rows = tokens.astype(jnp.float32).reshape(BUFFERS, TOK_DEV, D)
    valid_rows = jax.vmap(valid_of)(seq_lengths)
    grad_rows = cotangent.astype(jnp.float32).reshape(BUFFERS, TOK_DEV, D) * valid_rows[:, :, None]

    def forward(wq_full, wkv_full, wo_full, up_full, down_full, vec_full, inputs):
        low_weights = (low(wq_full), low(wkv_full), low(wo_full), low(up_full), low(down_full), low(vec_full))

        def visit_row(carried, element):
            return (carried, jax.checkpoint(row_forward)(low_weights, element[0], element[1]))
        unused, result = lax.scan(visit_row, jnp.float32(0.0), (inputs, seq_lengths))
        return result
    outputs, pullback = jax.vjp(forward, wq_master, wkv_master, wo_master, ffw_up_master, ffw_down_master, vec_master, x_rows)
    grad_q, grad_kv, grad_o, grad_up, grad_down, grad_vec, grad_x = pullback(grad_rows)
    block_out = outputs.reshape(TOKENS, D).astype(jnp.bfloat16)
    input_grad = grad_x.reshape(TOKENS, D).astype(jnp.bfloat16)
    squares = jnp.sum(grad_q * grad_q) + jnp.sum(grad_kv * grad_kv) + jnp.sum(grad_o * grad_o)
    squares = squares + jnp.sum(grad_up * grad_up) + jnp.sum(grad_down * grad_down) + jnp.sum(grad_vec * grad_vec)
    grad_norm = jnp.sqrt(squares)
    factor = jnp.minimum(1.0, CLIP_NORM / grad_norm)
    q_out = adamw(grad_q, wq_first, wq_second, wq_master, factor, D ** (-0.5))
    kv_out = adamw(grad_kv, wkv_first, wkv_second, wkv_master, factor, D ** (-0.5))
    o_out = adamw(grad_o, wo_first, wo_second, wo_master, factor, (H * HD // 32) ** (-0.5))
    up_out = adamw(grad_up, ffw_up_first, ffw_up_second, ffw_up_master, factor, D ** (-0.5))
    down_out = adamw(grad_down, ffw_down_first, ffw_down_second, ffw_down_master, factor, FF ** (-0.5))
    vec_out = adamw(grad_vec, vec_first, vec_second, vec_master, factor, LR_VECTOR)
    return (block_out, input_grad, grad_norm, q_out[0], q_out[1], q_out[2], q_out[3], q_out[4], kv_out[0], kv_out[1], kv_out[2], kv_out[3], kv_out[4], o_out[0], o_out[1], o_out[2], o_out[3], o_out[4], up_out[0], up_out[1], up_out[2], up_out[3], up_out[4], down_out[0], down_out[1], down_out[2], down_out[3], down_out[4], vec_out[0], vec_out[1], vec_out[2], vec_out[3], vec_out[4])
```

```python
import functools
import math

import jax
import jax.numpy as jnp
from jax import lax
from jax.experimental import pallas as pl
from jax.experimental.pallas import tpu as pltpu
from jax.sharding import PartitionSpec as P

D = 2560
H = 10
HD = 256
FF = 7680
WINDOW = 2048
STEP = 5


EPS_NORM = 1e-06
ROPE_BASE = 10000.0
NEG_BIG = -1e30
CLIP_NORM = 1.0
BETA_ONE = 0.5
BETA_TWO = 0.75
EPS_ADAM = 1e-08
DECAY_RATE = 0.1
LR_VECTOR = 0.3


def layout(lengths, tok_count):
    places = jnp.arange(tok_count, dtype=jnp.int32)
    end_at = jnp.cumsum(lengths)
    segment = jnp.sum((places[:, None] >= end_at[None, :]).astype(jnp.int32), axis=1)
    slot_ids = jnp.arange(lengths.shape[0], dtype=jnp.int32)
    start_of = jnp.sum(jnp.where(segment[:, None] > slot_ids[None, :], lengths[None, :], 0), axis=1)
    position = places - start_of
    valid_mask = (places < end_at[lengths.shape[0] - 1]).astype(jnp.float32)
    return (places, segment, position, valid_mask)


def angle_tables(position):
    half_dim = HD // 2
    quarter = half_dim // 2
    exponent = jnp.arange(quarter, dtype=jnp.float32) * (2.0 / half_dim)
    angles = position.astype(jnp.float32)[:, None] / (ROPE_BASE**exponent)[None, :]
    cosine = jnp.cos(angles)
    sine = jnp.sin(angles)
    return (
        jnp.concatenate([cosine, cosine], axis=1),
        jnp.concatenate([-sine, sine], axis=1),
    )


def turn(block, cosine, sine):
    quarter = block.shape[-1] // 2
    swapped = jnp.concatenate([block[..., quarter:], block[..., :quarter]], axis=-1)
    return block * cosine + swapped * sine


def shift(values, by):
    size = lax.axis_size("fsdp")
    return lax.ppermute(values, "fsdp", [(i, (i + by) % size) for i in range(size)])


def gather_near(values):
    size = lax.axis_size("fsdp")
    return (
        lax.ppermute(values, "fsdp", [(i, i + 1) for i in range(size - 1)]),
        lax.ppermute(values, "fsdp", [(i + 1, i) for i in range(size - 1)]),
    )


def gather_far(values, near):
    size = lax.axis_size("fsdp")
    here = lax.axis_index("fsdp")
    above, below = near
    from_above, from_below = [values, above], [values, below]
    for k in range(2, size):
        links = [(i, i + k - 1) for i in range(1, size - k + 1)]
        from_above.append(lax.ppermute(above, "fsdp", links))
        links = [(size - 1 - i, size - 1 - j) for i, j in links]
        from_below.append(lax.ppermute(below, "fsdp", links))
    return [values] + [
        jnp.where(here >= k, from_above[k], from_below[size - k]) for k in range(1, size)
    ]


def gather_group(values):
    return gather_far(values, gather_near(values))


def send_home(blocks):
    return [blocks[0]] + [shift(blocks[k], -k) for k in range(1, len(blocks))]


def send_out(blocks):
    return [blocks[0]] + [shift(blocks[k], k) for k in range(1, len(blocks))]


def pick(choices, which):
    result = choices[0]
    for i in range(1, len(choices)):
        result = jnp.where(which == i, choices[i], result)
    return result


def split_rows(values, parts):
    rows = values.shape[0] // parts
    return [values[k * rows : (k + 1) * rows] for k in range(parts)]


def split_cols(values, parts):
    cols = values.shape[1] // parts
    return [values[:, k * cols : (k + 1) * cols] for k in range(parts)]


def add_up(pieces):
    total = pieces[0].astype(jnp.float32)
    for piece in pieces[1:]:
        total = total + piece.astype(jnp.float32)
    return total


def attention_mask(info_ref, count, slots):
    rows = lax.broadcasted_iota(jnp.int32, (count, count), 0)
    cols = lax.broadcasted_iota(jnp.int32, (count, count), 1)
    end_at = 0
    same = None
    for s in range(slots):
        end_at = end_at + info_ref[1 + s]
        agree = (rows >= end_at) == (cols >= end_at)
        same = agree if same is None else same & agree
    return same & (cols <= rows) & (rows - cols < WINDOW)


def cost(multiply_adds, read_and_written):
    return pl.CostEstimate(
        flops=2 * multiply_adds, bytes_accessed=read_and_written, transcendentals=0
    )


def mxu(left, right, left_dim, right_dim):
    return lax.dot_general(
        left, right, (((left_dim,), (right_dim,)), ((), ())), preferred_element_type=jnp.float32
    )


def soft(queries, keys, allowed):
    scores = jnp.where(allowed, mxu(queries, keys, 1, 1), NEG_BIG)
    raised = jnp.exp(scores - jnp.max(scores, axis=1, keepdims=True))
    return raised / jnp.sum(raised, axis=1, keepdims=True)


def forward_kernel(slots, q_cols, info_ref, *refs):
    size = len(refs) - 3
    came, (att_ref, q_ref, kv_ref) = refs[:size], refs[size:]
    here = info_ref[0]
    kv_cols = came[0].shape[1] - q_cols
    for k in range(size):
        at = lax.rem(here + k, size)
        q_ref[:, pl.ds(pl.multiple_of(at * q_cols, 128), q_cols)] = came[k][:, :q_cols]
        kv_ref[:, pl.ds(pl.multiple_of(at * kv_cols, 128), kv_cols)] = came[k][:, q_cols:]
    allowed = attention_mask(info_ref, q_ref.shape[0], slots)
    keys = kv_ref[:, :HD]
    values = kv_ref[:, HD:]
    for h in range(H):
        probs = soft(q_ref[:, h * HD : (h + 1) * HD], keys, allowed)
        att_ref[:, h * HD : (h + 1) * HD] = mxu(
            probs.astype(jnp.bfloat16), values, 1, 0
        ).astype(jnp.bfloat16)


def backward_kernel(slots, q_cols, info_ref, q_ref, kv_ref, cos_ref, sin_ref, *refs):
    parts, out_ref = refs[:-1], refs[-1]
    low = jnp.bfloat16
    half = HD // 2
    size = out_ref.shape[0]
    here = info_ref[0]
    allowed = attention_mask(info_ref, q_ref.shape[0], slots)
    keys = kv_ref[:, :HD]
    values = kv_ref[:, HD:]
    cosine = cos_ref[...]
    sine = sin_ref[...]
    kv_cols = out_ref.shape[2] - q_cols
    key_grad = jnp.zeros((q_ref.shape[0], HD), jnp.float32)
    value_grad = jnp.zeros((q_ref.shape[0], HD), jnp.float32)

    def back(block):
        swapped = jnp.concatenate([block[:, half // 2 :], block[:, : half // 2]], axis=1)
        return block * cosine - swapped * sine

    def place(block, column, width, offset):
        entry = lax.rem(column // width - here + size, size)
        start = offset + column % width
        out_ref[entry, :, start : start + half] = block.astype(low)

    for h in range(H):
        cols = slice(h * HD, (h + 1) * HD)
        queries = q_ref[:, cols]
        grads = parts[0][:, cols].astype(jnp.float32)
        for part in parts[1:]:
            grads = grads + part[:, cols].astype(jnp.float32)
        grads = grads.astype(low)
        probs = soft(queries, keys, allowed)
        grad_prob = mxu(grads, values, 1, 1)
        value_grad = value_grad + mxu(probs.astype(low), grads, 0, 0)
        row_delta = jnp.sum(probs * grad_prob, axis=1, keepdims=True)
        grad_score = (probs * (grad_prob - row_delta)).astype(low)
        key_grad = key_grad + mxu(grad_score, queries, 0, 0)
        query_grad = mxu(grad_score, keys, 1, 0) * HD ** (-0.5)
        place(back(query_grad[:, :half]), h * HD, q_cols, 0)
        place(query_grad[:, half:], h * HD + half, q_cols, 0)
    place(back(key_grad[:, :half]), 0, kv_cols, q_cols)
    place(key_grad[:, half:], half, kv_cols, q_cols)
    place(value_grad[:, :half], HD, kv_cols, q_cols)
    place(value_grad[:, half:], HD + half, kv_cols, q_cols)


def kernel_specs(count):
    return [pl.BlockSpec(memory_space=pltpu.SMEM)] + [
        pl.BlockSpec(memory_space=pltpu.VMEM)
    ] * count


def attend(info, came, q_cols):
    rows = came[0].shape[0]
    slots = info.shape[0] - 1
    return pl.pallas_call(
        functools.partial(forward_kernel, slots, q_cols),
        out_shape=(
            jax.ShapeDtypeStruct((rows, H * HD), jnp.bfloat16),
            jax.ShapeDtypeStruct((rows, H * HD), jnp.bfloat16),
            jax.ShapeDtypeStruct((rows, 2 * HD), jnp.bfloat16),
        ),
        in_specs=kernel_specs(len(came)),
        out_specs=(pl.BlockSpec(memory_space=pltpu.VMEM),) * 3,
        compiler_params=pltpu.CompilerParams(vmem_limit_bytes=32 * 2**20),
    )(info, *came)


def attend_back(info, queries, keys_values, cosine, sine, parts, q_cols, kv_cols):
    rows = queries.shape[0]
    slots = info.shape[0] - 1
    size = len(parts)
    return pl.pallas_call(
        functools.partial(backward_kernel, slots, q_cols),
        out_shape=jax.ShapeDtypeStruct((size, rows, q_cols + kv_cols), jnp.bfloat16),
        in_specs=kernel_specs(4 + size),
        out_specs=pl.BlockSpec(memory_space=pltpu.VMEM),
        compiler_params=pltpu.CompilerParams(vmem_limit_bytes=32 * 2**20),
    )(info, queries, keys_values, cosine, sine, *parts)


def spread_kernel(place_ref, left_a, right_a, left_b, right_b, keep_ref, send_ref):
    rows = keep_ref.shape[1]
    width = right_a.shape[1]
    chunk = 640
    for c in range(left_a.shape[1] // chunk):
        cols = slice(c * chunk, (c + 1) * chunk)
        full_a = mxu(left_a[:, cols], right_a[...], 0, 0).astype(jnp.bfloat16)
        full_b = mxu(left_b[:, cols], right_b[...], 0, 0).astype(jnp.bfloat16)
        for t in range(chunk // rows):
            entry = jnp.bitwise_xor(c * (chunk // rows) + t, place_ref[0])
            at = lax.div(entry, 2)
            even = entry - 2 * at == 0
            block_a = full_a[t * rows : (t + 1) * rows]
            block_b = full_b[t * rows : (t + 1) * rows]

            @pl.when(even)
            def _():
                keep_ref[at, :, :width] = block_a
                keep_ref[at, :, width:] = block_b

            @pl.when(jnp.logical_not(even))
            def _():
                send_ref[at, :, :width] = block_a
                send_ref[at, :, width:] = block_b


def spread_products(place, left_a, right_a, left_b, right_b, count):
    features = left_a.shape[1]
    width = right_a.shape[1] + right_b.shape[1]
    shape = jax.ShapeDtypeStruct((count // 2, features // count, width), jnp.bfloat16)
    return pl.pallas_call(
        spread_kernel,
        out_shape=(shape, shape),
        in_specs=kernel_specs(4),
        out_specs=(pl.BlockSpec(memory_space=pltpu.VMEM),) * 2,
        cost_estimate=cost(left_a.size * width, 2 * features * width),
        compiler_params=pltpu.CompilerParams(vmem_limit_bytes=48 * 2**20),
    )(place, left_a, right_a, left_b, right_b)


def swap(values, mask):
    count = lax.axis_size("dp")
    return lax.ppermute(values, "dp", [(i, i ^ mask) for i in range(count)])


def add_low(one, two):
    return (one.astype(jnp.float32) + two.astype(jnp.float32)).astype(jnp.bfloat16)


def halve(part, order, beside):
    left = sorted(order, reverse=True)
    for bit in order:
        axis = left.index(bit)
        cube = part.reshape((2,) * len(left) + part.shape[-2:])
        stay = lax.index_in_dim(cube, 0, axis, keepdims=False)
        leave = lax.index_in_dim(cube, 1, axis, keepdims=False)
        if len(left) == len(order) and beside is not None:
            stay, beside = lax.optimization_barrier((stay, beside))
        part = add_low(stay, swap(leave, 2 << bit))
        left.remove(bit)
    return part, beside


ROOT = (2.0 / math.pi) ** 0.5
CUBE = 0.044715


def add_up_blocks(total, part):
    step = pl.program_id(0)

    @pl.when(step == 0)
    def _():
        total[...] = part

    @pl.when(step > 0)
    def _():
        total[...] += part


def feed_forward_kernel(
    info_ref, normed_ref, gate_w, up_w, down_w, gate_ref, up_ref, hidden_ref, out_ref, total
):
    gate_lin = mxu(normed_ref[...], gate_w[...], 1, 0)
    up_lin = mxu(normed_ref[...], up_w[...], 1, 0)
    gate_ref[...] = gate_lin
    up_ref[...] = up_lin
    bend = jnp.tanh(ROOT * (gate_lin + CUBE * gate_lin * gate_lin * gate_lin))
    hidden = (0.5 * gate_lin * (1.0 + bend) * up_lin).astype(jnp.bfloat16)
    hidden_ref[...] = hidden
    add_up_blocks(total, mxu(hidden, down_w[...], 1, 1))

    @pl.when(pl.program_id(0) == pl.num_programs(0) - 1)
    def _():
        size, rows, _ = out_ref.shape
        for k in range(size):
            owner = lax.rem(info_ref[0] - k + size, size)
            out_ref[owner] = total[k * rows : (k + 1) * rows, :].astype(out_ref.dtype)


def feed_back_kernel(grad_ref, gate_lin, up_lin, down_w, gate_ref, lin_ref):
    hidden_grad = mxu(grad_ref[...], down_w[...], 1, 0)
    gate = gate_lin[...]
    square = gate * gate
    bend = jnp.tanh(ROOT * (gate + CUBE * square * gate))
    half = 0.5 * (1.0 + bend)
    slope = half + 0.5 * gate * (1.0 - bend * bend) * (ROOT * (1.0 + 3 * CUBE * square))
    gate_ref[...] = (hidden_grad * up_lin[...] * slope).astype(jnp.bfloat16)
    lin_ref[...] = (hidden_grad * (gate * half)).astype(jnp.bfloat16)


def back_product_kernel(gate_ref, lin_ref, gate_w, up_w, *out_refs):
    part = mxu(gate_ref[...], gate_w[...], 1, 1) + mxu(lin_ref[...], up_w[...], 1, 1)
    rows = part.shape[0] // len(out_refs)
    for k, out_ref in enumerate(out_refs):
        out_ref[...] = part[k * rows : (k + 1) * rows, :].astype(out_ref.dtype)


def unit_blocks(rows, weights):
    features, width = weights.shape
    units = width // 3
    step = 640 if units % 640 == 0 else 384
    steps = units // step
    whole = pl.BlockSpec((rows, features), lambda i: (0, 0), pipeline_mode=pl.Buffered(1))
    part = pl.BlockSpec((rows, step), lambda i: (0, i))
    blocks = [
        pl.BlockSpec((features, step), lambda i, at=at: (0, i + at * steps)) for at in range(3)
    ]
    return units, steps, whole, part, blocks


def feed_forward(info, normed, weights, size):
    rows, features = normed.shape
    units, steps, whole, part, blocks = unit_blocks(rows, weights)
    low = jnp.bfloat16
    result = pl.pallas_call(
        feed_forward_kernel,
        grid=(steps,),
        out_shape=(jax.ShapeDtypeStruct((rows, units), jnp.float32),) * 2
        + (
            jax.ShapeDtypeStruct((rows, units), low),
            pltpu.HBM((size, rows // size, 2 * features), low),
        ),
        in_specs=[pl.BlockSpec(memory_space=pltpu.SMEM), whole, *blocks],
        out_specs=(part,) * 3
        + (pl.BlockSpec((size, rows // size, features), lambda i: (0, 0, 0)),),
        scratch_shapes=[pltpu.VMEM((rows, features), jnp.float32)],
        cost_estimate=cost(3 * rows * features * units, 2 * weights.size + 14 * rows * units),
        compiler_params=pltpu.CompilerParams(vmem_limit_bytes=58 * 2**20),
    )(info, normed, weights, weights, weights)
    return result


def feed_back(grads, gate_lin, up_lin, weights):
    rows, features = grads.shape
    units, steps, whole, part, blocks = unit_blocks(rows, weights)
    return pl.pallas_call(
        feed_back_kernel,
        grid=(steps,),
        out_shape=(jax.ShapeDtypeStruct((rows, units), jnp.bfloat16),) * 2,
        in_specs=[whole, part, part, blocks[2]],
        out_specs=(part,) * 2,
        cost_estimate=cost(rows * features * units, 2 * features * units + 12 * rows * units),
        compiler_params=pltpu.CompilerParams(vmem_limit_bytes=58 * 2**20),
    )(grads, gate_lin, up_lin, weights)


def back_product(gate_low, lin_low, weights, half, size):
    rows, units = gate_low.shape
    features = weights.shape[0] // 2
    step = 640
    start = half * (features // step)
    whole = pl.BlockSpec((rows, units), lambda i: (0, 0), pipeline_mode=pl.Buffered(1))
    return list(
        pl.pallas_call(
            back_product_kernel,
            grid=(features // step,),
            out_shape=(jax.ShapeDtypeStruct((rows // size, features), jnp.bfloat16),) * size,
            in_specs=[
                whole,
                whole,
                pl.BlockSpec((step, units), lambda i: (i + start, 0)),
                pl.BlockSpec((step, units), lambda i: (i + start, 1)),
            ],
            out_specs=(pl.BlockSpec((rows // size, step), lambda i: (0, i)),) * size,
            cost_estimate=cost(2 * rows * features * units, 4 * features * units),
            compiler_params=pltpu.CompilerParams(vmem_limit_bytes=58 * 2**20),
        )(gate_low, lin_low, weights, weights)
    )


def last_product_kernel(info_ref, grad_ref, w_ref, token_ref, inverse_ref, _, out_ref, gain_ref):
    part = mxu(grad_ref[...], w_ref[...], 1, 1)
    scaled = part * (token_ref[...].astype(jnp.float32) * inverse_ref[...])
    gain_ref[...] = jnp.sum(scaled, axis=0, keepdims=True)
    size, rows, _ = out_ref.shape
    for k in range(size):
        owner = lax.rem(info_ref[0] - k + size, size)
        out_ref[owner] = part[k * rows : (k + 1) * rows, :].astype(out_ref.dtype)


def last_product(info, grads, weights, tokens, inverse, wide):
    rows, features = tokens.shape
    step = 640
    start = features // step
    size = wide.shape[0]
    return pl.pallas_call(
        last_product_kernel,
        grid=(features // step,),
        out_shape=(
            pltpu.HBM(wide.shape, wide.dtype),
            jax.ShapeDtypeStruct((1, features), jnp.float32),
        ),
        in_specs=[
            pl.BlockSpec(memory_space=pltpu.SMEM),
            pl.BlockSpec(grads.shape, lambda i: (0, 0)),
            pl.BlockSpec((step, grads.shape[1]), lambda i: (i, 0)),
            pl.BlockSpec((rows, step), lambda i: (0, i)),
            pl.BlockSpec((rows, 1), lambda i: (0, 0)),
            pl.BlockSpec(memory_space=pltpu.HBM),
        ],
        out_specs=(
            pl.BlockSpec((size, rows // size, step), lambda i: (0, 0, i + start)),
            pl.BlockSpec((1, step), lambda i: (0, i)),
        ),
        input_output_aliases={5: 0},
        cost_estimate=cost(rows * features * grads.shape[1], 6 * rows * features),
        compiler_params=pltpu.CompilerParams(vmem_limit_bytes=32 * 2**20),
    )(info, grads, weights, tokens, inverse, wide)


def product_kernel(left_ref, *refs):
    out_ref = refs[-1]
    start = 0
    for right_ref in refs[:-1]:
        width = right_ref.shape[1]
        out_ref[:, start : start + width] = mxu(left_ref[...], right_ref[...], 0, 0).astype(
            out_ref.dtype
        )
        start += width


def product(left, *rights):
    rows, features = left.shape
    step = 640
    width = sum(right.shape[1] for right in rights)
    return pl.pallas_call(
        product_kernel,
        grid=(features // step,),
        out_shape=jax.ShapeDtypeStruct((features, width), jnp.bfloat16),
        in_specs=[pl.BlockSpec((rows, step), lambda i: (0, i))]
        + [
            pl.BlockSpec(right.shape, lambda i: (0, 0), pipeline_mode=pl.Buffered(1))
            for right in rights
        ],
        out_specs=pl.BlockSpec((step, width), lambda i: (i, 0)),
        cost_estimate=cost(rows * features * width, 2 * features * width),
        compiler_params=pltpu.CompilerParams(vmem_limit_bytes=58 * 2**20),
    )(left, *rights)


def update_kernel(rates, factor_ref, o_ref, qkv_ref, up_ref, down_ref, *refs):
    count = len(rates)
    factor = factor_ref[0, 0]
    sources = (o_ref, qkv_ref, qkv_ref, up_ref, down_ref)
    start = 0
    for m in range(count):
        first, second, weight = refs[m], refs[count + m], refs[2 * count + m]
        outs = refs[3 * count + 5 * m : 3 * count + 5 * (m + 1)]
        parts = [()] if len(weight.shape) == 2 else [(p,) for p in range(weight.shape[0])]
        width = weight.shape[-1]
        if m == 0 or sources[m] is not sources[m - 1]:
            start = 0
        for part in parts:
            gradient = sources[m][:, start : start + width].astype(jnp.float32)
            start += width
            results = adamw(
                gradient, first[part + (...,)], second[part + (...,)], weight[part + (...,)],
                factor, rates[m],
            )
            for out, result in zip(outs, results):
                out[part + (...,)] = result


def update(factor, gradients, masters, firsts, seconds, rates):
    rows = gradients[0].shape[0]
    step = 32 if rows % 32 == 0 else 16

    def spec(shape):
        if len(shape) == 2:
            return pl.BlockSpec((step, shape[1]), lambda i: (i, 0))
        return pl.BlockSpec((shape[0], step, shape[2]), lambda i: (0, i, 0))

    states = (*firsts, *seconds, *masters)
    out_shape, out_specs = [], []
    for master in masters:
        for kind in (jnp.float32,) * 4 + (jnp.bfloat16,):
            out_shape.append(jax.ShapeDtypeStruct(master.shape, kind))
            out_specs.append(spec(master.shape))
    result = pl.pallas_call(
        functools.partial(update_kernel, rates),
        grid=(rows // step,),
        out_shape=out_shape,
        in_specs=[pl.BlockSpec(memory_space=pltpu.SMEM)]
        + [spec(g.shape) for g in gradients]
        + [spec(one.shape) for one in states],
        out_specs=out_specs,
        cost_estimate=cost(0, sum(10 * m.size for m in states)),
        compiler_params=pltpu.CompilerParams(vmem_limit_bytes=58 * 2**20),
    )(factor.reshape(1, 1), *gradients, *states)
    return [result[5 * m : 5 * m + 5] for m in range(len(masters))]


def sum_along(axis, values):
    size = lax.axis_size(axis)
    step = 1
    while step < size:
        values = values + lax.ppermute(values, axis, [(i, i ^ step) for i in range(size)])
        step *= 2
    return values


def sum_everywhere(values):
    return sum_along("dp", sum_along("fsdp", values))


def adamw(gradient, first_mom, second_mom, weight, factor, step_rate):
    clipped = gradient * factor
    first_new = BETA_ONE * first_mom + (1.0 - BETA_ONE) * clipped
    second_new = BETA_TWO * second_mom + (1.0 - BETA_TWO) * clipped * clipped
    first_hat = first_new / (1.0 - BETA_ONE**STEP)
    second_hat = second_new / (1.0 - BETA_TWO**STEP)
    weight_new = weight - step_rate * (
        first_hat / (jnp.sqrt(second_hat) + EPS_ADAM) + DECAY_RATE * weight
    )
    return (clipped, first_new, second_new, weight_new, weight_new.astype(jnp.bfloat16))


def body(
    tokens,
    cotangent,
    seq_lengths,
    wq_master,
    wkv_master,
    wo_master,
    ffw_up_master,
    ffw_down_master,
    vec_master,
    wq_first,
    wq_second,
    wkv_first,
    wkv_second,
    wo_first,
    wo_second,
    ffw_up_first,
    ffw_up_second,
    ffw_down_first,
    ffw_down_second,
    vec_first,
    vec_second,
):
    size = lax.axis_size("fsdp")
    here = lax.axis_index("fsdp")
    owner = lax.axis_index("dp") * size + here
    tok_count = tokens.shape[0]
    vec_cols = vec_master.shape[1]
    q_cols = wq_master.shape[1]
    kv_cols = wkv_master.shape[1]
    low = jnp.bfloat16
    contract_rows = (((0,), (0,)), ((), ()))
    contract_cols = (((1,), (1,)), ((), ()))

    def dot(left, right):
        return jnp.dot(left, right, preferred_element_type=jnp.float32)

    def dot_rows(left, right):
        return lax.dot_general(left, right, contract_rows, preferred_element_type=jnp.float32)

    def dot_cols(left, right):
        return lax.dot_general(left, right, contract_cols, preferred_element_type=jnp.float32)

    attn_weights = lax.all_gather(
        jnp.concatenate([wq_master, wkv_master, wo_master], axis=1).astype(low),
        "dp",
        axis=0,
        tiled=True,
    )
    units = ffw_up_master.shape[2]
    qkv_full = attn_weights[:, : q_cols + kv_cols]
    wo_cols = attn_weights[:, q_cols + kv_cols :]

    token_near = gather_near(tokens)

    slots = seq_lengths.shape[1]
    small = jnp.zeros((8, 128), jnp.float32)
    small = lax.dynamic_update_slice(small, vec_master.astype(low).astype(jnp.float32), (0, 0))
    small = lax.dynamic_update_slice(small, seq_lengths.astype(jnp.float32), (4, 0))
    small_blocks = [small] + [shift(small, k) for k in range(1, size)]
    length_blocks = [b[4, :slots].astype(jnp.int32) for b in small_blocks]
    vec_low = jnp.zeros((4, D), jnp.float32)
    for k in range(size):
        block_at = owner - here + (here - k) % size
        vec_low = lax.dynamic_update_slice(
            vec_low, small_blocks[k][:4, :vec_cols], (0, block_at * vec_cols)
        )
    up_master, down_master, vec_low = lax.optimization_barrier(
        (ffw_up_master, ffw_down_master, vec_low)
    )
    ffw_shard = jnp.concatenate(
        [up_master[0].astype(low), up_master[1].astype(low), down_master.T.astype(low)], axis=1
    )
    vec_low = sum_along("dp", vec_low)
    vec_low, token_near, ffw_shard = lax.optimization_barrier((vec_low, token_near, ffw_shard))
    ffw_weights = lax.all_gather(ffw_shard, "dp", axis=0, tiled=True)

    token_blocks = gather_far(tokens, token_near)
    gain_one, bias_one, gain_two, bias_two = (vec_low[i : i + 1] for i in range(4))
    group_tokens = jnp.concatenate(token_blocks, axis=0)
    places, segment, position, valid_mask = layout(seq_lengths[0], tok_count)
    valid_col = valid_mask[:, None]
    group_position = jnp.concatenate([layout(b, tok_count)[2] for b in length_blocks])
    grad_out = cotangent.astype(jnp.float32) * valid_col
    grad_low, group_tokens = lax.optimization_barrier((grad_out.astype(low), group_tokens))
    grad_near = gather_near(grad_low)
    x_group = group_tokens.astype(jnp.float32)
    group_inverse = lax.rsqrt(jnp.mean(x_group * x_group, axis=1, keepdims=True) + EPS_NORM)
    normed = (x_group * group_inverse * gain_one).astype(low)
    qkv_lin = dot(normed, qkv_full)
    group_cos, group_sin = angle_tables(group_position)
    half_dim = HD // 2
    turned = []
    for b in range((q_cols + kv_cols) // half_dim):
        block = qkv_lin[:, b * half_dim : (b + 1) * half_dim]
        if b * half_dim < q_cols:
            rotated = (here * (q_cols // half_dim) + b) % 2 == 0
            scale = HD ** (-0.5)
        else:
            rotated = here * (kv_cols // half_dim) + b - q_cols // half_dim == 0
            scale = 1.0
        turned.append((jnp.where(rotated, turn(block, group_cos, group_sin), block) * scale).astype(low))
    qkv_low = jnp.concatenate(turned, axis=1)
    came = send_home(split_rows(qkv_low, size))
    came, grad_near = lax.optimization_barrier((came, grad_near))

    def in_order(pieces):
        return jnp.concatenate([pick(pieces, (j - here) % size) for j in range(size)], axis=1)

    info = jnp.concatenate([here.astype(jnp.int32)[None], seq_lengths[0]])
    attended, queries, keys_values = attend(info, came, q_cols)
    group_attended = jnp.concatenate(gather_group(attended), axis=0)
    branch = dot(group_attended, wo_cols).astype(low)
    branch = in_order(send_home(split_rows(branch, size))).astype(jnp.float32)
    x_float = tokens.astype(jnp.float32)
    inverse = group_inverse[:tok_count]
    mixed = x_float + valid_col * (branch + bias_one)
    inv_two = lax.rsqrt(jnp.mean(mixed * mixed, axis=1, keepdims=True) + EPS_NORM)
    normed_two = (mixed * inv_two * gain_two).astype(low)
    group_normed = jnp.concatenate(gather_group(normed_two), axis=0)

    grad_near, group_normed, ffw_weights = lax.optimization_barrier(
        (grad_near, group_normed, ffw_weights)
    )
    group_grad = jnp.concatenate(gather_far(grad_low, grad_near), axis=0)

    gate_lin, up_lin, hidden, ffw_part = feed_forward(info, group_normed, ffw_weights, size)
    group_grad, ffw_part = lax.optimization_barrier((group_grad, ffw_part))
    down_grad = product(group_grad, hidden)
    own_down = lax.psum_scatter(down_grad, "dp", scatter_dimension=0, tiled=True)
    group_grad, down_grad = lax.optimization_barrier((group_grad, down_grad))
    gate_low, lin_low = feed_back(group_grad, gate_lin, up_lin, ffw_weights)
    first_pieces = send_home(back_product(gate_low, lin_low, ffw_weights, 0, size))
    second_pieces = send_home(back_product(gate_low, lin_low, ffw_weights, 1, size))
    gate_last, first_pieces = lax.optimization_barrier((gate_low, first_pieces))
    up_grad = product(group_normed, gate_last, lin_low)
    up_grad, second_pieces = lax.optimization_barrier((up_grad, second_pieces))
    normed_two_grad = jnp.concatenate([add_up(first_pieces), add_up(second_pieces)], axis=1)
    own_up = lax.psum_scatter(up_grad, "dp", scatter_dimension=0, tiled=True)
    bias_two_grad = jnp.sum(grad_out, axis=0)

    gain_two_grad = jnp.sum(normed_two_grad * mixed * inv_two, axis=0)
    scaled_two = normed_two_grad * gain_two
    mixed_grad = (
        inv_two
        * (
            scaled_two
            - mixed * inv_two * inv_two * jnp.mean(scaled_two * mixed, axis=1, keepdims=True)
        )
        + grad_out
    )
    branch_low = (mixed_grad * valid_col).astype(low)
    bias_one_grad = jnp.sum(branch_low.astype(jnp.float32), axis=0)

    def column_blocks(values):
        blocks = split_cols(values, size)
        return [pick(blocks, (here + k) % size) for k in range(size)]

    branch_cols = jnp.concatenate(send_out(column_blocks(branch_low)), axis=0)
    attn_part = dot_cols(branch_cols, wo_cols).astype(low)
    place = lax.axis_index("dp").astype(jnp.int32)[None]
    dp_size = lax.axis_size("dp")
    attn_pieces = send_home(split_rows(attn_part, size))
    outgoing = attend_back(
        info,
        queries,
        keys_values,
        group_cos[:tok_count],
        group_sin[:tok_count],
        attn_pieces,
        q_cols,
        kv_cols,
    )
    qkv_grad = jnp.concatenate(send_out([outgoing[k] for k in range(size)]), axis=0)
    keep, send = spread_products(place, group_attended, branch_cols, normed, qkv_grad, dp_size)
    got = swap(send, 1)
    wide, gain_one_grad = last_product(
        info, qkv_grad, attn_weights, group_tokens, group_inverse, ffw_part
    )
    wide, got = lax.optimization_barrier((wide, got))
    last_sums = lax.psum_scatter(
        wide.reshape(size * tok_count, 2 * D), "fsdp", scatter_dimension=0, tiled=True
    )

    def square_sum(values):
        values = values.astype(jnp.float32)
        return jnp.sum(values * values)

    ffw_squares = square_sum(own_down) + square_sum(own_up)
    total = add_low(keep, got)
    bits = list(range(keep.shape[0].bit_length() - 1))
    own_o, _ = halve(total[:, :, :q_cols], bits, ffw_squares)
    own_qkv, ffw_squares = halve(total[:, :, q_cols:], bits[::-1], ffw_squares)
    vec_grad = sum_everywhere(
        jnp.stack([gain_one_grad[0], bias_one_grad, gain_two_grad, bias_two_grad])
    )
    def square_sum(values):
        values = values.astype(jnp.float32)
        return jnp.sum(values * values)

    squares = square_sum(own_down) + square_sum(own_up)
    own_vec = lax.dynamic_slice(vec_grad, (0, owner * vec_cols), (4, vec_cols))

    squares = ffw_squares + square_sum(own_o) + square_sum(own_qkv)
    squares = sum_along("fsdp", sum_along("dp", jnp.broadcast_to(squares, (8, 128))))[0, 0]
    grad_norm = jnp.sqrt(squares + jnp.sum(vec_grad * vec_grad))
    factor = jnp.minimum(1.0, CLIP_NORM / grad_norm)
    o_out, q_out, kv_out, up_out, down_out = update(
        factor,
        (own_o, own_qkv, own_up, own_down),
        (wo_master, wq_master, wkv_master, ffw_up_master, ffw_down_master.T),
        (wo_first, wq_first, wkv_first, ffw_up_first, ffw_down_first.T),
        (wo_second, wq_second, wkv_second, ffw_up_second, ffw_down_second.T),
        ((H * HD // 32) ** (-0.5), D ** (-0.5), D ** (-0.5), D ** (-0.5), FF ** (-0.5)),
    )
    last_sums, down_out = lax.optimization_barrier((last_sums, down_out))
    ffw_term = last_sums[:, :D].astype(jnp.float32)
    block_out = (mixed + valid_col * (ffw_term + bias_two)).astype(low)
    normed_grad = last_sums[:, D:]
    scaled = normed_grad.astype(jnp.float32) * gain_one
    input_grad = (
        inverse
        * (scaled - x_float * inverse * inverse * jnp.mean(scaled * x_float, axis=1, keepdims=True))
        + mixed_grad
    ).astype(low)
    down_out = [one.T for one in down_out]
    vec_out = adamw(own_vec, vec_first, vec_second, vec_master, factor, LR_VECTOR)
    return (
        block_out,
        input_grad,
        grad_norm,
        q_out[0],
        q_out[1],
        q_out[2],
        q_out[3],
        q_out[4],
        kv_out[0],
        kv_out[1],
        kv_out[2],
        kv_out[3],
        kv_out[4],
        o_out[0],
        o_out[1],
        o_out[2],
        o_out[3],
        o_out[4],
        up_out[0],
        up_out[1],
        up_out[2],
        up_out[3],
        up_out[4],
        down_out[0],
        down_out[1],
        down_out[2],
        down_out[3],
        down_out[4],
        vec_out[0],
        vec_out[1],
        vec_out[2],
        vec_out[3],
        vec_out[4],
    )


def solution(mesh):
    placed = (
        P(("dp", "fsdp"), None),
        P(("dp", "fsdp"), None),
        P(("dp", "fsdp"), None),
        P("dp", "fsdp"),
        P("dp", "fsdp"),
        P("dp", "fsdp"),
        P(None, "dp", "fsdp"),
        P("fsdp", "dp"),
        P(None, ("dp", "fsdp")),
        P("dp", "fsdp"),
        P("dp", "fsdp"),
        P("dp", "fsdp"),
        P("dp", "fsdp"),
        P("dp", "fsdp"),
        P("dp", "fsdp"),
        P(None, "dp", "fsdp"),
        P(None, "dp", "fsdp"),
        P("fsdp", "dp"),
        P("fsdp", "dp"),
        P(None, ("dp", "fsdp")),
        P(None, ("dp", "fsdp")),
    )
    return jax.shard_map(
        body,
        mesh=mesh,
        in_specs=placed,
        out_specs=(
            P(("dp", "fsdp"), None),
            P(("dp", "fsdp"), None),
            P(),
            P("dp", "fsdp"),
            P("dp", "fsdp"),
            P("dp", "fsdp"),
            P("dp", "fsdp"),
            P("dp", "fsdp"),
            P("dp", "fsdp"),
            P("dp", "fsdp"),
            P("dp", "fsdp"),
            P("dp", "fsdp"),
            P("dp", "fsdp"),
            P("dp", "fsdp"),
            P("dp", "fsdp"),
            P("dp", "fsdp"),
            P("dp", "fsdp"),
            P("dp", "fsdp"),
            P(None, "dp", "fsdp"),
            P(None, "dp", "fsdp"),
            P(None, "dp", "fsdp"),
            P(None, "dp", "fsdp"),
            P(None, "dp", "fsdp"),
            P("fsdp", "dp"),
            P("fsdp", "dp"),
            P("fsdp", "dp"),
            P("fsdp", "dp"),
            P("fsdp", "dp"),
            P(None, ("dp", "fsdp")),
            P(None, ("dp", "fsdp")),
            P(None, ("dp", "fsdp")),
            P(None, ("dp", "fsdp")),
            P(None, ("dp", "fsdp")),
        ),
        check_vma=False,
    )
```
